32 devices in a mesh: row: 8 (over z, core), col: 4 (over y, x).
Axes of the slice: x: 2, y: 2, z: 4, core: 2. Of those that a mesh axis runs over, the one named last changes fastest.
Arguments:
- factor: bfloat16 [28672, 28672], P('row', 'col'), may hold values from -8 to 50
- subspace: bfloat16 [28672, 1024], P(('col', 'row')), may hold values from -6 to 6
Outputs:
- new_basis: float32 [28672, 1024], P(('row', 'col'))
- r_factor: float32 [1024, 1024], replicated
The draws below stay inside these ranges and needn't reach their ends.
All inputs are finite; a program needn't handle non-finite values.
Results may differ from the reference program's by a relative error of at most 0.0009.
Values may be sent and summed in bfloat16 or wider, within the bound.
No kernel may reach another device: no remote copies, remote signals or barrier semaphores. Data moves between devices by JAX's collectives and lax.ppermute only.
A program may use at most 192 MiB of HBM per device.

```python
import math
import jax
import jax.numpy as jnp
from jax import lax

N = 28672
K = 1024


def draw_factor(key, part):
    key_noise, key_scale = jax.random.split(jax.random.fold_in(key, 17))
    position = jnp.arange(N)
    jitter = jnp.clip(jax.random.normal(key_noise, (N, N), jnp.float32), -6.0, 6.0)
    row_scale = jnp.exp(jax.random.uniform(key_scale, (N,), jnp.float32, 0.0, math.log(10.0)))
    row_scale = row_scale * jnp.exp(math.log(3.0) * position.astype(jnp.float32) / N)
    side_scale = jnp.sqrt(row_scale)
    mirrored = (jitter + jitter.T) * 0.5
    identity = (position[:, None] == position[None, :]).astype(jnp.float32)
    entries = mirrored * (0.5 / math.sqrt(N)) + identity
    return (side_scale[:, None] * entries * side_scale[None, :]).astype(jnp.bfloat16)


def level_of(rng, shape, cuts, smallest, top_value):
    gain = 1.0
    for axis_at, blocks in cuts:
        draws = jax.random.uniform(jax.random.fold_in(jax.random.fold_in(rng, 6), axis_at), (blocks,), jnp.float32, smallest / len(cuts), top_value / len(cuts))
        gain = gain * jnp.repeat(jnp.exp(draws), shape[axis_at] // blocks).reshape((-1,) + (1,) * (len(shape) - 1 - axis_at))
    return gain


def bell_draw(key, shape, deviation, reach, pieces=(), dtype=jnp.bfloat16):
    loudness = level_of(key, shape, pieces, -0.22, 0.18) if pieces else 1.0
    drawn = jax.random.normal(key, shape, jnp.float32) * deviation * loudness
    return jnp.minimum(jnp.maximum(drawn, -reach), reach).astype(dtype)


def setup_inputs(seed: int = 0) -> dict:
    key_list = jax.random.split(jax.random.key(seed), 3)
    return {
        "factor": draw_factor(jax.random.fold_in(key_list[2], 71), 0),
        "subspace": bell_draw(key_list[1], (N, K), 1.0, 6.0, ((0, 32),)),
    }


def reference(factor, subspace):
    block_rows = min(N, 1024)
    blocks = factor.reshape(N // block_rows, block_rows, N)

    def block_product(rows_block):
        return jnp.dot(rows_block.astype(jnp.float32), subspace.astype(jnp.float32), preferred_element_type=jnp.float32)
    image = lax.map(block_product, blocks).reshape(N, K)
    gram_matrix = jnp.dot(image.T, image, precision=lax.Precision.HIGHEST) / N
    symmetric = (gram_matrix + gram_matrix.T) / 2.0
    lower_factor = jnp.linalg.cholesky(symmetric)
    solved = lax.linalg.triangular_solve(lower_factor, image.T, left_side=True, lower=True)
    return (solved.T, lower_factor.T)
```

```python
import functools

import jax
import jax.numpy as jnp
from jax import lax
from jax.experimental import pallas as pl
from jax.experimental.pallas import tpu as pltpu
from jax.sharding import PartitionSpec as P

WIDTHS = (256, 256, 256, 256)
PIVOTS = 128
TILE = 8
HIGHEST = lax.Precision.HIGHEST


def gather_rows(block, cores, size):
    levels = size // cores
    index = lax.axis_index("row")
    level, core = index // cores, index % cores
    rows = block.shape[0]
    swap = [(i, i ^ 1) for i in range(size)]
    up = [(i, i + cores) for i in range(size - cores)]
    down = [(i + cores, i) for i in range(size - cores)]

    rising, falling = [block], [block]
    for _ in range(levels - 1):
        rising.append(lax.ppermute(rising[-1], "row", up))
        falling.append(lax.ppermute(falling[-1], "row", down))
    panel = jnp.zeros((size, rows, block.shape[1]), block.dtype)

    def put(panel, piece, slot):
        return lax.dynamic_update_slice(panel, piece[None], (slot, 0, 0))

    other = [lax.ppermute(block, "row", swap)]
    panel = put(panel, block, index)
    panel = put(panel, other[0], level * cores + 1 - core)
    rising_other = [None] + [lax.ppermute(p, "row", swap) for p in rising[1:]]
    falling_other = [None] + [lax.ppermute(p, "row", swap) for p in falling[1:]]
    for step in range(1, levels):
        slot = (level - step + levels) % levels * cores
        from_below = level >= step
        mine = jnp.where(from_below, rising[step], falling[levels - step])
        theirs = jnp.where(from_below, rising_other[step], falling_other[levels - step])
        panel = put(panel, mine, slot + core)
        panel = put(panel, theirs, slot + 1 - core)
    return panel.reshape(size * rows, block.shape[1])


def exchange_columns(partial, size):
    rows = partial.shape[0] // size
    width = partial.shape[1]
    index = lax.axis_index("col")
    pieces = partial.reshape(size, rows, width)
    top = jnp.max(jnp.abs(pieces), axis=1)
    exponent = jnp.ceil(jnp.log2(jnp.maximum(top, 1e-30)))
    total = lax.dynamic_index_in_dim(pieces, index, 0, keepdims=False)
    for step in range(1, size):
        to = (index + step) % size
        piece = lax.dynamic_index_in_dim(pieces, to, 0, keepdims=False)
        power = lax.dynamic_index_in_dim(exponent, to, 0, keepdims=True)
        coded = (piece * jnp.exp2(14.0 - power)).astype(jnp.float16)
        tail = jnp.broadcast_to(power, (16, width)).astype(jnp.float16)
        sent = jnp.concatenate([coded, tail], axis=0)
        got = lax.ppermute(sent, "col", [(i, (i + step) % size) for i in range(size)])
        got = got.astype(jnp.float32)
        total = total + got[:rows] * jnp.exp2(got[rows : rows + 1] - 14.0)
    return total


def scatter_axis(block, axis, size, index, perm):
    rows = block.shape[0] // size
    total = lax.dynamic_slice_in_dim(block, index * rows, rows, 0)
    for step in range(1, size):
        piece = lax.dynamic_slice_in_dim(block, (index + step) % size * rows, rows, 0)
        total = total + lax.ppermute(piece, axis, perm(step))
    return total


def gather_axis(block, axis, size, index, perm):
    rows = block.shape[0]
    whole = jnp.zeros((size * rows, block.shape[1]), block.dtype)
    whole = lax.dynamic_update_slice_in_dim(whole, block, index * rows, 0)
    for step in range(1, size):
        got = lax.ppermute(block, axis, perm(step))
        whole = lax.dynamic_update_slice_in_dim(whole, got, (index - step + size) % size * rows, 0)
    return whole


def sum_everywhere(block, cores, row_size, col_size):
    levels = row_size // cores
    row = lax.axis_index("row")
    level, core = row // cores, row % cores
    col = lax.axis_index("col")
    core_perm = lambda step: [(i, i // cores * cores + (i + step) % cores) for i in range(row_size)]
    col_perm = lambda step: [(i, (i + step) % col_size) for i in range(col_size)]
    level_perm = lambda step: [(i, (i + step * cores) % row_size) for i in range(row_size)]
    stages = (("row", cores, core, core_perm), ("col", col_size, col, col_perm), ("row", levels, level, level_perm))
    for axis, size, index, perm in stages:
        block = scatter_axis(block, axis, size, index, perm)
    for axis, size, index, perm in reversed(stages):
        block = gather_axis(block, axis, size, index, perm)
    return block


def eliminate(block):
    groups = PIVOTS // TILE
    lane = lax.broadcasted_iota(jnp.int32, (TILE, PIVOTS), 1)
    sub = lax.broadcasted_iota(jnp.int32, (TILE, PIVOTS), 0)
    held = [block[g * TILE : (g + 1) * TILE] for g in range(groups)]
    factor, inverse = [], []
    for g in range(groups):
        for i in range(TILE):
            j = g * TILE + i
            at = lane == j
            row = jnp.broadcast_to(held[g][i : i + 1], (TILE, PIVOTS))
            pivot = jnp.broadcast_to(row[:, j : j + 1], (TILE, PIVOTS))
            scaled = jnp.where(at, 1.0, row) / pivot
            for h in range(g, groups):
                if h == g and i == TILE - 1:
                    continue
                weight = jnp.broadcast_to(held[h][:, j : j + 1], (TILE, PIVOTS))
                new = jnp.where(at, 0.0, held[h]) - weight * scaled
                held[h] = jnp.where(sub > i, new, held[h]) if h == g else new
        own = sub + g * TILE
        diagonal = jnp.sum(jnp.where(lane == own, held[g], 0.0), axis=1, keepdims=True)
        root = lax.rsqrt(diagonal)
        root = root * (1.5 - 0.5 * diagonal * root * root)
        factor.append(jnp.where(lane >= own, held[g] * root, 0.0))
        inverse.append(jnp.where(lane < own, held[g] * root, jnp.where(lane == own, root, 0.0)))
    return jnp.concatenate(factor, 0), jnp.concatenate(inverse, 0)


def mul(a, b):
    return jnp.dot(a, b, precision=HIGHEST, preferred_element_type=jnp.float32)


def column_kernel(scale, before, width, gram_ref, *refs):
    factor_ref, inverse_ref = refs[-2:]
    block = gram_ref[before:, :] * scale
    if before:
        above = mul(refs[0][...], gram_ref[:before, :] * scale)
        factor_ref[:before, :] = above
        above_t = above.T
        block = block - mul(above_t, above)
    block = (block + block.T) * 0.5
    if width == PIVOTS:
        factor, inverse = eliminate(block)
    else:
        first, first_inverse = eliminate(block[:PIVOTS, :PIVOTS])
        corner = mul(first_inverse, block[:PIVOTS, PIVOTS:])
        corner_t = corner.T
        last, last_inverse = eliminate(block[PIVOTS:, PIVOTS:] - mul(corner_t, corner))
        low = -mul(last_inverse, mul(corner_t, first_inverse))
        none = jnp.zeros((PIVOTS, PIVOTS), jnp.float32)
        factor = jnp.concatenate(
            [jnp.concatenate([first, corner], 1), jnp.concatenate([none, last], 1)], 0
        )
        inverse = jnp.concatenate(
            [jnp.concatenate([first_inverse, none], 1), jnp.concatenate([low, last_inverse], 1)], 0
        )
    factor_ref[before:, :] = factor
    inverse_ref[:, before:] = inverse
    if before:
        inverse_ref[:, :before] = -mul(mul(inverse, above_t), refs[0][...])


def factor_column(gram, inverse_before, scale):
    width = gram.shape[1]
    before = gram.shape[0] - width
    operands = (gram,) if inverse_before is None else (gram, inverse_before)
    return pl.pallas_call(
        functools.partial(column_kernel, scale, before, width),
        out_shape=(
            jax.ShapeDtypeStruct((before + width, width), jnp.float32),
            jax.ShapeDtypeStruct((width, before + width), jnp.float32),
        ),
        in_specs=[pl.BlockSpec(memory_space=pltpu.VMEM)] * len(operands),
        out_specs=(pl.BlockSpec(memory_space=pltpu.VMEM),) * 2,
        compiler_params=pltpu.CompilerParams(vmem_limit_bytes=32 * 1024 * 1024),
        cost_estimate=pl.CostEstimate(flops=20_000_000_000, bytes_accessed=4_000_000, transcendentals=0),
    )(*operands)


def body(row_size, col_size, cores, factor, subspace):
    total_rows = factor.shape[1] * col_size
    scale = 1.0 / total_rows
    images, bases, columns = [], [], []
    inverse = None
    start = 0
    for width in WIDTHS:
        with jax.named_scope(f"chunk{start}"):
            panel = gather_rows(lax.slice_in_dim(subspace, start, start + width, axis=1), cores, row_size)
            partial = jnp.dot(factor, panel, preferred_element_type=jnp.float32)
            images.append(exchange_columns(partial, col_size))
            so_far = jnp.concatenate(images, axis=1)
            gram = lax.dot_general(
                so_far, images[-1], (((0,), (0,)), ((), ())), precision=HIGHEST, preferred_element_type=jnp.float32
            )
            gram = sum_everywhere(gram, cores, row_size, col_size)
            column, last_rows = factor_column(gram, inverse, scale)
            bases.append(
                lax.dot_general(
                    so_far, last_rows, (((1,), (1,)), ((), ())), precision=lax.Precision.HIGH, preferred_element_type=jnp.float32
                )
            )
            if inverse is None:
                inverse = last_rows
            else:
                inverse = jnp.concatenate([jnp.pad(inverse, ((0, 0), (0, width))), last_rows], axis=0)
            start += width
            columns.append(jnp.pad(column, ((0, subspace.shape[1] - start), (0, 0))))
    return jnp.concatenate(bases, axis=1), jnp.concatenate(columns, axis=1)


def solution(mesh):
    row_size, col_size = mesh.shape["row"], mesh.shape["col"]
    return jax.shard_map(
        functools.partial(body, row_size, col_size, 2),
        mesh=mesh,
        in_specs=(P("row", "col"), P(("col", "row"), None)),
        out_specs=(P(("row", "col"), None), P()),
        check_vma=False,
    )
```

```python
import functools

import jax
import jax.numpy as jnp
from jax import lax
from jax.experimental import pallas as pl
from jax.experimental.pallas import tpu as pltpu
from jax.sharding import PartitionSpec as P

WIDTHS = (512, 256, 256)
COLUMN = 256
PIVOTS = 128
TILE = 8
CORES = 2
ROW_TILE = 448
HIGHEST = lax.Precision.HIGHEST


class Timeline:
    def __init__(self):
        self.now = 0
        self.values = {}
        self.due = {}

    def put(self, key, value, at):
        self.values[key] = value
        self.due.setdefault(max(at, self.now + 1), []).append(key)

    def get(self, key):
        return self.values[key]

    def advance(self):
        self.now += 1
        keys = self.due.pop(self.now, [])
        passed = lax.optimization_barrier(tuple(self.values[k] for k in keys))
        self.values.update(zip(keys, passed))


def line_slots(chunks, steps):
    sent, arrival = {}, {}
    for i, step in enumerate(line_order(chunks, steps)):
        if step and step[0] == 0:
            whole = i + 1
    for i, step in enumerate(line_order(chunks, steps)):
        if step and i - 1 < whole:
            sent[step], arrival[step] = max(i - 1, 0), i + 1
    slot = whole
    while len(sent) < chunks * steps:
        able = []
        for c in range(chunks):
            step = next((k for k in range(1, steps + 1) if (c, k) not in sent), None)
            if step and (step == 1 or arrival[c, step - 1] <= slot):
                able.append((c, step))
        for step in able[:2]:
            sent[step], arrival[step] = slot, slot + 1
        slot += 1
    return sent, arrival


def line_order(chunks, steps):
    order, taken, last = [], [0] * chunks, [-2] * chunks
    while min(taken) < steps:
        able = [c for c in range(chunks) if taken[c] < steps and last[c] <= len(order) - 2]
        if not able:
            order.append(None)
            continue
        c = min(able, key=lambda c: (c * (steps - 1) + taken[c], -c))
        last[c] = len(order)
        taken[c] += 1
        order.append((c, taken[c]))
    return order


def product_kernel(levels, pieces, place_ref, factor_ref, *refs):
    blocks, (out_ref, panel_ref, sems) = refs[:-3], refs[-3:]
    level, core = place_ref[pieces], place_ref[pieces + 1]
    rows = blocks[0].shape[0]
    own, rising, falling = blocks[:2], blocks[2 : 2 * levels], blocks[2 * levels :]

    @pl.when((pl.program_id(0) == 0) & (pl.program_id(1) == 0))
    def _():
        def copy(block, slot, sem):
            start = pl.multiple_of(slot * rows, 16)
            return pltpu.make_async_copy(block, panel_ref.at[pl.ds(start, rows)], sems.at[sem])

        waits = []
        for swapped in range(2):
            at_core = (1 - core) if swapped else core
            first = copy(own[swapped], level * CORES + at_core, swapped)
            first.start()
            waits.append(first)
            for step in range(1, levels):
                slot = (level - step + levels) % levels * CORES + at_core
                sem = 2 * step + swapped
                below = copy(rising[2 * (step - 1) + swapped], slot, sem)
                above = copy(falling[2 * (levels - step - 1) + swapped], slot, sem)

                @pl.when(level >= step)
                def _():
                    below.start()

                @pl.when(level < step)
                def _():
                    above.start()

                waits.append(below)
        for wait in waits:
            wait.wait()

    out_ref[0] = jnp.dot(factor_ref[...], panel_ref[...], preferred_element_type=jnp.float32)


def product(factor, blocks, levels, place, pieces, rows):
    tile = rows
    while tile > ROW_TILE:
        tile //= 2
    per = rows // tile
    depth = factor.shape[1]
    width = blocks[0].shape[1]
    return pl.pallas_call(
        functools.partial(product_kernel, levels, pieces),
        out_shape=jax.ShapeDtypeStruct((pieces, rows, width), jnp.float32),
        grid_spec=pltpu.PrefetchScalarGridSpec(
            num_scalar_prefetch=1,
            grid=(pieces, per),
            in_specs=[pl.BlockSpec((tile, depth), lambda p, t, place: (place[p] * per + t, 0))]
            + [pl.BlockSpec(memory_space=pl.ANY)] * len(blocks),
            out_specs=pl.BlockSpec((1, tile, width), lambda p, t, place: (p, t, 0)),
            scratch_shapes=[
                pltpu.VMEM((depth, width), factor.dtype),
                pltpu.SemaphoreType.DMA((2 * levels,)),
            ],
        ),
        compiler_params=pltpu.CompilerParams(vmem_limit_bytes=30 * 1024 * 1024),
        cost_estimate=pl.CostEstimate(
            flops=2 * pieces * rows * depth * width, bytes_accessed=2 * pieces * rows * depth, transcendentals=0
        ),
    )(place, factor, *blocks)


def encode(piece):
    top = jnp.max(jnp.abs(piece), axis=0, keepdims=True)
    power = jnp.ceil(jnp.log2(jnp.maximum(top, 1e-30)))
    coded = (piece * jnp.exp2(14.0 - power)).astype(jnp.float16)
    tail = jnp.broadcast_to(power, (16, piece.shape[1])).astype(jnp.float16)
    return jnp.concatenate([coded, tail], axis=0)


def decode(sent):
    sent = sent.astype(jnp.float32)
    rows = sent.shape[0] - 16
    return sent[:rows] * jnp.exp2(sent[rows : rows + 1] - 14.0)


def inverse_of(x):
    guess = pl.reciprocal(x, approx=True)
    return guess * (2.0 - x * guess)


def eliminate(block):
    groups = PIVOTS // TILE
    shape = (TILE, PIVOTS)
    lane = lax.broadcasted_iota(jnp.int32, shape, 1)
    sub = lax.broadcasted_iota(jnp.int32, shape, 0)
    held = [block[g * TILE : (g + 1) * TILE] for g in range(groups)]
    factor, inverse = [], []
    for g in range(groups):
        base = g * TILE
        inside = (lane >= base) & (lane < base + TILE)
        rows = [jnp.broadcast_to(held[g][i : i + 1], shape) for i in range(TILE)]
        entry = [
            [jnp.broadcast_to(rows[i][:, base + j : base + j + 1], shape) if j >= i else None for j in range(TILE)]
            for i in range(TILE)
        ]
        upper = list(rows)
        unit = [jnp.where(inside, jnp.where(lane == base + i, 1.0, 0.0), rows[i]) for i in range(TILE)]
        pivot_inverse = []
        lower = [[None] * TILE for _ in range(TILE)]
        for k in range(TILE):
            pivot_inverse.append(inverse_of(entry[k][k]))
            for i in range(k + 1, TILE):
                weight = entry[k][i] * pivot_inverse[k]
                lower[i][k] = weight
                for j in range(i, TILE):
                    entry[i][j] = entry[i][j] - weight * entry[k][j]
                upper[i] = upper[i] - weight * upper[k]
                unit[i] = unit[i] - weight * unit[k]
        solved = [None] * TILE
        for k in reversed(range(TILE)):
            value = unit[k] * pivot_inverse[k]
            for i in range(k + 1, TILE):
                value = value - lower[i][k] * solved[i]
            solved[k] = value
        for h in range(g + 1, groups):
            old = held[h]
            new = jnp.where(inside, 0.0, old)
            for k in range(TILE):
                new = new - jnp.broadcast_to(old[:, base + k : base + k + 1], shape) * solved[k]
            held[h] = new
        diagonal, top, low = entry[0][0], upper[0], unit[0]
        for k in range(1, TILE):
            diagonal = jnp.where(sub == k, entry[k][k], diagonal)
            top = jnp.where(sub == k, upper[k], top)
            low = jnp.where(sub == k, unit[k], low)
        root = lax.rsqrt(diagonal)
        root = root * (1.5 - 0.5 * diagonal * root * root)
        own = sub + base
        factor.append(jnp.where(lane >= own, top * root, 0.0))
        inverse.append(jnp.where(lane <= own, low * root, 0.0))
    return jnp.concatenate(factor, 0), jnp.concatenate(inverse, 0)


def mul(a, b):
    return jnp.dot(a, b, precision=HIGHEST, preferred_element_type=jnp.float32)


def column_kernel(scale, before, width, gram_ref, *refs):
    factor_ref, inverse_ref = refs[-2:]
    block = gram_ref[before:, :] * scale
    if before:
        above = mul(refs[0][...], gram_ref[:before, :] * scale)
        factor_ref[:before, :] = above
        above_t = above.T
        block = block - mul(above_t, above)
    block = (block + block.T) * 0.5
    if width == PIVOTS:
        factor, inverse = eliminate(block)
    else:
        first, first_inverse = eliminate(block[:PIVOTS, :PIVOTS])
        corner = mul(first_inverse, block[:PIVOTS, PIVOTS:])
        corner_t = corner.T
        last, last_inverse = eliminate(block[PIVOTS:, PIVOTS:] - mul(corner_t, corner))
        low = -mul(last_inverse, mul(corner_t, first_inverse))
        none = jnp.zeros((PIVOTS, PIVOTS), jnp.float32)
        factor = jnp.concatenate(
            [jnp.concatenate([first, corner], 1), jnp.concatenate([none, last], 1)], 0
        )
        inverse = jnp.concatenate(
            [jnp.concatenate([first_inverse, none], 1), jnp.concatenate([low, last_inverse], 1)], 0
        )
    factor_ref[before:, :] = factor
    inverse_ref[:, before:] = inverse
    if before:
        inverse_ref[:, :before] = -mul(mul(inverse, above_t), refs[0][...])


def factor_column(gram, inverse_before, scale):
    width = gram.shape[1]
    before = gram.shape[0] - width
    operands = (gram,) if inverse_before is None else (gram, inverse_before)
    return pl.pallas_call(
        functools.partial(column_kernel, scale, before, width),
        out_shape=(
            jax.ShapeDtypeStruct((before + width, width), jnp.float32),
            jax.ShapeDtypeStruct((width, before + width), jnp.float32),
        ),
        in_specs=[pl.BlockSpec(memory_space=pltpu.VMEM)] * len(operands),
        out_specs=(pl.BlockSpec(memory_space=pltpu.VMEM),) * 2,
        compiler_params=pltpu.CompilerParams(vmem_limit_bytes=32 * 1024 * 1024),
        cost_estimate=pl.CostEstimate(flops=16_000_000_000, bytes_accessed=4_000_000, transcendentals=0),
    )(*operands)


def body(row_size, col_size, factor, subspace):
    rows = subspace.shape[0]
    total_rows = rows * row_size * col_size
    levels = row_size // CORES
    chunks = len(WIDTHS)
    starts = [sum(WIDTHS[:c]) for c in range(chunks)]
    row, col = lax.axis_index("row"), lax.axis_index("col")
    level, core = row // CORES, row % CORES
    up = [(i, i + CORES) for i in range(row_size - CORES)]
    down = [(i + CORES, i) for i in range(row_size - CORES)]
    swap = [(i, i // CORES * CORES + (i + 1) % CORES) for i in range(row_size)]

    line = Timeline()
    put, get = line.put, line.get
    tasks = {}

    def at(slot, task):
        tasks.setdefault(slot, []).append(task)

    sent, arrival = line_slots(chunks, levels - 1)

    def send_line(c, step):
        def task():
            for way, perm in (("up", up), ("down", down)):
                source = get((way, c, step - 1)) if step > 1 else get(("own", c))
                put((way, c, step), lax.ppermute(source, "row", perm), arrival[c, step])

        return task

    def swap_cores(c, step, due):
        def task():
            for way in ("up", "down") if step else ("own",):
                key = (way, c, step) if step else (way, c)
                value = lax.ppermute(get(key), "row", swap)
                if due is None:
                    line.values[("swap",) + key] = value
                else:
                    put(("swap",) + key, value, due)

        return task

    for c, width in enumerate(WIDTHS):
        own = lax.slice_in_dim(subspace, starts[c], starts[c] + width, axis=1)
        put(("own", c), own, sent[c, 1])
        at(sent[c, 1], swap_cores(c, 0, arrival[c, 1]))
        for step in range(1, levels):
            at(sent[c, step], send_line(c, step))
            last = step == levels - 1
            at(arrival[c, step], swap_cores(c, step, None if last else arrival[c, step] + 1))

    def parts_of(c):
        calls = min(1 if 0 < c < chunks - 1 else 2, col_size)
        return [(col_size * i // calls, col_size * (i + 1) // calls) for i in range(calls)]

    def assemble(c):
        def task():
            blocks = [get(("own", c)), get(("swap", "own", c))]
            for way in ("up", "down"):
                for step in range(1, levels):
                    blocks += [get((way, c, step)), get(("swap", way, c, step))]
            line.values["blocks", c] = blocks

        return task

    def multiply(c, part):
        def task():
            low, high = part
            value = product(factor, get(("blocks", c)), levels, get(("place", c, part)), high - low, rows)
            put(("product", c, part), value, line.now + 1)

        return task

    def send_pieces(c, part, due):
        def task():
            value = get(("product", c, part))
            for p in range(*part):
                piece = value[p - part[0]]
                if p == col_size - 1:
                    line.values["kept", c] = piece
                else:
                    perm = [(i, (i + p + 1) % col_size) for i in range(col_size)]
                    put(("got", c, p), lax.ppermute(encode(piece), "col", perm), due)

        return task

    def add_pieces(c):
        def task():
            total = get(("kept", c))
            for p in range(col_size - 1):
                total = total + decode(get(("got", c, p)))
            line.values["image", c] = total
            images = [get(("image", i)) for i in range(c + 1)]
            line.values["so far", c] = jnp.concatenate(images, axis=1) if c else total

        return task

    stages = (
        ("row", CORES, core, lambda step: [(i, i // CORES * CORES + (i + step) % CORES) for i in range(row_size)]),
        ("col", col_size, col, lambda step: [(i, (i + step) % col_size) for i in range(col_size)]),
        ("row", levels, level, lambda step: [(i, (i + step * CORES) % row_size) for i in range(row_size)]),
    )

    def inner_products(c):
        def task():
            line.values["sum", c] = lax.dot_general(
                get(("so far", c)),
                get(("image", c)),
                (((0,), (0,)), ((), ())),
                precision=HIGHEST,
                preferred_element_type=jnp.float32,
            )

        return task

    def scatter_send(c, stage):
        def task():
            axis, size, index, perm = stages[stage]
            block = get(("sum", c))
            part = block.shape[0] // size
            for step in range(1, size):
                piece = lax.dynamic_slice_in_dim(block, (index + step) % size * part, part, 0)
                put(("add", c, step), lax.ppermute(piece, axis, perm(step)), line.now + 1)

        return task

    def scatter_add(c, stage):
        def task():
            _, size, index, _ = stages[stage]
            block = get(("sum", c))
            part = block.shape[0] // size
            total = lax.dynamic_slice_in_dim(block, index * part, part, 0)
            for step in range(1, size):
                total = total + get(("add", c, step))
            line.values["sum", c] = total

        return task

    def gather_send(c, stage):
        def task():
            axis, size, _, perm = stages[stage]
            for step in range(1, size):
                put(("add", c, step), lax.ppermute(get(("sum", c)), axis, perm(step)), line.now + 1)

        return task

    def gather_put(c, stage):
        def task():
            _, size, index, _ = stages[stage]
            block = get(("sum", c))
            part = block.shape[0]
            whole = jnp.zeros((size * part, block.shape[1]), block.dtype)
            whole = lax.dynamic_update_slice_in_dim(whole, block, index * part, 0)
            for step in range(1, size):
                whole = lax.dynamic_update_slice_in_dim(
                    whole, get(("add", c, step)), (index - step + size) % size * part, 0
                )
            line.values["sum", c] = whole

        return task


    def finish(c):
        def task():
            gram, inverse = get(("sum", c)), line.values.get("inverse")
            for low in range(0, WIDTHS[c], COLUMN):
                end = starts[c] + low + COLUMN
                column, last_rows = factor_column(gram[:end, low : low + COLUMN], inverse, 1.0 / total_rows)
                line.values["column", end] = jnp.pad(column, ((0, subspace.shape[1] - end), (0, 0)))
                if inverse is None:
                    inverse = last_rows
                else:
                    inverse = jnp.concatenate([jnp.pad(inverse, ((0, 0), (0, COLUMN))), last_rows], axis=0)
            line.values["inverse"] = inverse
            put(("last", c), inverse[starts[c] :], line.now + 1)

        return task

    def multiply_basis(c):
        def task():
            line.values["basis", c] = lax.dot_general(
                get(("so far", c)),
                get(("last", c)),
                (((1,), (1,)), ((), ())),
                precision=lax.Precision.HIGH,
                preferred_element_type=jnp.float32,
            )

        return task

    busy = 0
    for c in range(chunks):
        ready = max(arrival[c, levels - 1], busy)
        at(ready, assemble(c))
        parts = parts_of(c)
        lag = 1 if c == chunks - 1 else 2
        for i, part in enumerate(parts):
            place = jnp.stack([(col + 1 + p) % col_size for p in range(*part)] + [level, core]).astype(jnp.int32)
            put(("place", c, part), place, ready + i)
            at(ready + i, multiply(c, part))
            at(ready + i + 1, send_pieces(c, part, ready + len(parts) + lag))
        busy = ready + len(parts)
        slot = busy + lag
        at(slot, add_pieces(c))
        at(slot, inner_products(c))
        for stage in range(len(stages)):
            at(slot, scatter_send(c, stage))
            at(slot + 1, scatter_add(c, stage))
            slot += 1
        for stage in reversed(range(len(stages))):
            at(slot, gather_send(c, stage))
            at(slot + 1, gather_put(c, stage))
            slot += 1
        at(slot, finish(c))
        at(slot + 1, multiply_basis(c))

    for slot in range(max(tasks) + 1):
        if slot:
            line.advance()
        for task in tasks.get(slot, []):
            task()
    basis = jnp.concatenate([get(("basis", c)) for c in range(chunks)], axis=1)
    upper = jnp.concatenate(
        [get(("column", end)) for end in range(COLUMN, subspace.shape[1] + 1, COLUMN)], axis=1
    )
    return basis, upper


def solution(mesh):
    row_size, col_size = mesh.shape["row"], mesh.shape["col"]
    return jax.shard_map(
        functools.partial(body, row_size, col_size),
        mesh=mesh,
        in_specs=(P("row", "col"), P(("col", "row"), None)),
        out_specs=(P(("row", "col"), None), P()),
        check_vma=False,
    )
```

```python
import functools

import jax
import jax.numpy as jnp
from jax import lax
from jax.experimental import pallas as pl
from jax.experimental.pallas import tpu as pltpu
from jax.sharding import PartitionSpec as P

WIDTHS = (512, 512)
COLUMN = 256
PIVOTS = 128
TILE = 8
BASE = (1, 1)
CORES = 2
ROW_TILE = 448
HIGHEST = lax.Precision.HIGHEST


class Timeline:
    def __init__(self):
        self.now = 0
        self.values = {}
        self.due = {}

    def put(self, key, value, at):
        self.values[key] = value
        self.due.setdefault(max(at, self.now + 1), []).append(key)

    def get(self, key):
        return self.values[key]

    def advance(self):
        self.now += 1
        keys = self.due.pop(self.now, [])
        passed = lax.optimization_barrier(tuple(self.values[k] for k in keys))
        self.values.update(zip(keys, passed))


def arrivals(levels):
    table = []
    for level in range(levels):
        came = []
        for step in range(1, levels):
            came += [("up", step)] if level >= step else []
            came += [("down", step)] if level + step < levels else []
        table.append(came)
    return table


def level_kernel(pieces, candidates, has_total, place_ref, factor_ref, *refs):
    blocks, (out_ref, panel_ref, sems) = refs[: 2 * candidates], refs[-3:]
    choice, core = place_ref[pieces + 1], place_ref[pieces + 2]
    rows = blocks[0].shape[0]

    @pl.when((pl.program_id(0) == 0) & (pl.program_id(1) == 0))
    def _():
        waits = []
        for swapped in range(2):
            start = pl.multiple_of(((1 - core) if swapped else core) * rows, 16)
            copies = [
                pltpu.make_async_copy(blocks[2 * k + swapped], panel_ref.at[pl.ds(start, rows)], sems.at[swapped])
                for k in range(candidates)
            ]
            for k, copy in enumerate(copies):

                @pl.when(choice == k)
                def _():
                    copy.start()

            waits.append(copies[0])
        for wait in waits:
            wait.wait()

    value = jnp.dot(factor_ref[...], panel_ref[...], preferred_element_type=jnp.float32)
    out_ref[0] = value + refs[2 * candidates][0] if has_total else value


def level_product(factor, blocks, total, place, part, rows):
    low, high = part
    pieces = high - low
    tile = rows
    while tile > ROW_TILE:
        tile //= 2
    per = rows // tile
    depth = CORES * rows
    width = blocks[0].shape[1]
    totals = [] if total is None else [total]
    whole = total is not None and total.shape[0] == pieces
    return pl.pallas_call(
        functools.partial(level_kernel, pieces, len(blocks) // 2, bool(totals)),
        out_shape=jax.ShapeDtypeStruct((pieces, rows, width), jnp.float32),
        grid_spec=pltpu.PrefetchScalarGridSpec(
            num_scalar_prefetch=1,
            grid=(pieces, per),
            in_specs=[pl.BlockSpec((tile, depth), lambda p, t, place: (place[p] * per + t, place[pieces]))]
            + [pl.BlockSpec(memory_space=pl.ANY)] * len(blocks)
            + [pl.BlockSpec((1, tile, width), lambda p, t, place: (p + low, t, 0))] * len(totals),
            out_specs=pl.BlockSpec((1, tile, width), lambda p, t, place: (p, t, 0)),
            scratch_shapes=[
                pltpu.VMEM((depth, width), factor.dtype),
                pltpu.SemaphoreType.DMA((2,)),
            ],
        ),
        input_output_aliases={2 + len(blocks): 0} if whole else {},
        compiler_params=pltpu.CompilerParams(vmem_limit_bytes=24 * 1024 * 1024),
        cost_estimate=pl.CostEstimate(
            flops=2 * pieces * rows * depth * width, bytes_accessed=2 * pieces * rows * depth, transcendentals=0
        ),
    )(place, factor, *blocks, *totals)


def product_kernel(levels, pieces, place_ref, factor_ref, *refs):
    blocks, (out_ref, panel_ref, sems) = refs[:-3], refs[-3:]
    level, core = place_ref[pieces], place_ref[pieces + 1]
    rows = blocks[0].shape[0]
    own, rising, falling = blocks[:2], blocks[2 : 2 * levels], blocks[2 * levels :]

    @pl.when((pl.program_id(0) == 0) & (pl.program_id(1) == 0))
    def _():
        def copy(block, slot, sem):
            start = pl.multiple_of(slot * rows, 16)
            return pltpu.make_async_copy(block, panel_ref.at[pl.ds(start, rows)], sems.at[sem])

        waits = []
        for swapped in range(2):
            at_core = (1 - core) if swapped else core
            first = copy(own[swapped], level * CORES + at_core, swapped)
            first.start()
            waits.append(first)
            for step in range(1, levels):
                slot = (level - step + levels) % levels * CORES + at_core
                sem = 2 * step + swapped
                below = copy(rising[2 * (step - 1) + swapped], slot, sem)
                above = copy(falling[2 * (levels - step - 1) + swapped], slot, sem)

                @pl.when(level >= step)
                def _():
                    below.start()

                @pl.when(level < step)
                def _():
                    above.start()

                waits.append(below)
        for wait in waits:
            wait.wait()

    out_ref[0] = jnp.dot(factor_ref[...], panel_ref[...], preferred_element_type=jnp.float32)


def product(factor, blocks, levels, place, pieces, rows):
    tile = rows
    while tile > ROW_TILE:
        tile //= 2
    per = rows // tile
    depth = factor.shape[1]
    width = blocks[0].shape[1]
    return pl.pallas_call(
        functools.partial(product_kernel, levels, pieces),
        out_shape=jax.ShapeDtypeStruct((pieces, rows, width), jnp.float32),
        grid_spec=pltpu.PrefetchScalarGridSpec(
            num_scalar_prefetch=1,
            grid=(pieces, per),
            in_specs=[pl.BlockSpec((tile, depth), lambda p, t, place: (place[p] * per + t, 0))]
            + [pl.BlockSpec(memory_space=pl.ANY)] * len(blocks),
            out_specs=pl.BlockSpec((1, tile, width), lambda p, t, place: (p, t, 0)),
            scratch_shapes=[
                pltpu.VMEM((depth, width), factor.dtype),
                pltpu.SemaphoreType.DMA((2 * levels,)),
            ],
        ),
        compiler_params=pltpu.CompilerParams(vmem_limit_bytes=30 * 1024 * 1024),
        cost_estimate=pl.CostEstimate(
            flops=2 * pieces * rows * depth * width, bytes_accessed=2 * pieces * rows * depth, transcendentals=0
        ),
    )(place, factor, *blocks)


def encode(piece):
    top = jnp.max(jnp.abs(piece), axis=0, keepdims=True)
    power = jnp.ceil(jnp.log2(jnp.maximum(top, 1e-30)))
    coded = (piece * jnp.exp2(14.0 - power)).astype(jnp.float16)
    tail = jnp.broadcast_to(power, (16, piece.shape[1])).astype(jnp.float16)
    return jnp.concatenate([coded, tail], axis=0)


def decode(sent):
    sent = sent.astype(jnp.float32)
    rows = sent.shape[0] - 16
    return sent[:rows] * jnp.exp2(sent[rows : rows + 1] - 14.0)


def inverse_of(x):
    guess = pl.reciprocal(x, approx=True)
    return guess * (2.0 - x * guess)


def eliminate(block):
    groups = PIVOTS // TILE
    shape = (TILE, PIVOTS)
    lane = lax.broadcasted_iota(jnp.int32, shape, 1)
    sub = lax.broadcasted_iota(jnp.int32, shape, 0)
    held = [block[g * TILE : (g + 1) * TILE] for g in range(groups)]
    factor, inverse = [], []
    for g in range(groups):
        base = g * TILE
        inside = (lane >= base) & (lane < base + TILE)
        rows = [jnp.broadcast_to(held[g][i : i + 1], shape) for i in range(TILE)]
        entry = [
            [jnp.broadcast_to(rows[i][:, base + j : base + j + 1], shape) if j >= i else None for j in range(TILE)]
            for i in range(TILE)
        ]
        upper = list(rows)
        unit = [jnp.where(inside, jnp.where(lane == base + i, 1.0, 0.0), rows[i]) for i in range(TILE)]
        pivot_inverse = []
        lower = [[None] * TILE for _ in range(TILE)]
        for k in range(TILE):
            pivot_inverse.append(inverse_of(entry[k][k]))
            for i in range(k + 1, TILE):
                weight = entry[k][i] * pivot_inverse[k]
                lower[i][k] = weight
                for j in range(i, TILE):
                    entry[i][j] = entry[i][j] - weight * entry[k][j]
                upper[i] = upper[i] - weight * upper[k]
                unit[i] = unit[i] - weight * unit[k]
        solved = [None] * TILE
        for k in reversed(range(TILE)):
            value = unit[k] * pivot_inverse[k]
            for i in range(k + 1, TILE):
                value = value - lower[i][k] * solved[i]
            solved[k] = value
        for h in range(g + 1, groups):
            old = held[h]
            new = jnp.where(inside, 0.0, old)
            for k in range(TILE):
                new = new - jnp.broadcast_to(old[:, base + k : base + k + 1], shape) * solved[k]
            held[h] = new
        diagonal, top, low = entry[0][0], upper[0], unit[0]
        for k in range(1, TILE):
            diagonal = jnp.where(sub == k, entry[k][k], diagonal)
            top = jnp.where(sub == k, upper[k], top)
            low = jnp.where(sub == k, unit[k], low)
        root = lax.rsqrt(diagonal)
        root = root * (1.5 - 0.5 * diagonal * root * root)
        own = sub + base
        factor.append(jnp.where(lane >= own, top * root, 0.0))
        inverse.append(jnp.where(lane <= own, low * root, 0.0))
    return jnp.concatenate(factor, 0), jnp.concatenate(inverse, 0)


def mul(a, b):
    return jnp.dot(a, b, precision=HIGHEST, preferred_element_type=jnp.float32)


def column_kernel(scale, before, width, gram_ref, *refs):
    factor_ref, inverse_ref = refs[-2:]
    block = gram_ref[before:, :] * scale
    if before:
        above = mul(refs[0][...], gram_ref[:before, :] * scale)
        factor_ref[:before, :] = above
        above_t = above.T
        block = block - mul(above_t, above)
    block = (block + block.T) * 0.5
    if width == PIVOTS:
        factor, inverse = eliminate(block)
    else:
        first, first_inverse = eliminate(block[:PIVOTS, :PIVOTS])
        corner = mul(first_inverse, block[:PIVOTS, PIVOTS:])
        corner_t = corner.T
        last, last_inverse = eliminate(block[PIVOTS:, PIVOTS:] - mul(corner_t, corner))
        low = -mul(last_inverse, mul(corner_t, first_inverse))
        none = jnp.zeros((PIVOTS, PIVOTS), jnp.float32)
        factor = jnp.concatenate(
            [jnp.concatenate([first, corner], 1), jnp.concatenate([none, last], 1)], 0
        )
        inverse = jnp.concatenate(
            [jnp.concatenate([first_inverse, none], 1), jnp.concatenate([low, last_inverse], 1)], 0
        )
    factor_ref[before:, :] = factor
    inverse_ref[:, before:] = inverse
    if before:
        inverse_ref[:, :before] = -mul(mul(inverse, above_t), refs[0][...])


def factor_column(gram, inverse_before, scale):
    width = gram.shape[1]
    before = gram.shape[0] - width
    operands = (gram,) if inverse_before is None else (gram, inverse_before)
    return pl.pallas_call(
        functools.partial(column_kernel, scale, before, width),
        out_shape=(
            jax.ShapeDtypeStruct((before + width, width), jnp.float32),
            jax.ShapeDtypeStruct((width, before + width), jnp.float32),
        ),
        in_specs=[pl.BlockSpec(memory_space=pltpu.VMEM)] * len(operands),
        out_specs=(pl.BlockSpec(memory_space=pltpu.VMEM),) * 2,
        compiler_params=pltpu.CompilerParams(vmem_limit_bytes=32 * 1024 * 1024),
        cost_estimate=pl.CostEstimate(flops=16_000_000_000, bytes_accessed=4_000_000, transcendentals=0),
    )(*operands)


def body(row_size, col_size, factor, subspace):
    rows = subspace.shape[0]
    total_rows = rows * row_size * col_size
    levels = row_size // CORES
    chunks = len(WIDTHS)
    starts = [sum(WIDTHS[:c]) for c in range(chunks)]
    row, col = lax.axis_index("row"), lax.axis_index("col")
    level, core = row // CORES, row % CORES
    up = [(i, i + CORES) for i in range(row_size - CORES)]
    down = [(i + CORES, i) for i in range(row_size - CORES)]
    swap = [(i, i // CORES * CORES + (i + 1) % CORES) for i in range(row_size)]

    line = Timeline()
    put, get = line.put, line.get
    tasks = {}

    def at(slot, task):
        tasks.setdefault(slot, []).append(task)

    sent = {(c, step): c * (levels - 2) + step - 1 for c in range(chunks) for step in range(1, levels)}
    arrival = {key: slot + 1 for key, slot in sent.items()}

    def send_line(c, step):
        def task():
            for way, perm in (("up", up), ("down", down)):
                source = get((way, c, step - 1)) if step > 1 else get(("own", c))
                put((way, c, step), lax.ppermute(source, "row", perm), arrival[c, step])

        return task

    def swap_cores(c, step):
        def task():
            for key in [("up", c, step), ("down", c, step)] if step else [("own", c)]:
                line.values[("swap",) + key] = lax.ppermute(get(key), "row", swap)

        return task

    for c, width in enumerate(WIDTHS):
        own = lax.slice_in_dim(subspace, starts[c], starts[c] + width, axis=1)
        put(("own", c), own, sent[c, 1])
        at(sent[c, 1], swap_cores(c, 0))
        for step in range(1, levels):
            at(sent[c, step], send_line(c, step))
            at(arrival[c, step], swap_cores(c, step))

    def parts_of(c):
        calls = min(1 if c < chunks - 1 else 2, col_size)
        return [(col_size * i // calls, col_size * (i + 1) // calls) for i in range(calls)]

    def assemble(c):
        def task():
            blocks = [get(("own", c)), get(("swap", "own", c))]
            for way in ("up", "down"):
                for step in range(1, levels):
                    blocks += [get((way, c, step)), get(("swap", way, c, step))]
            line.values["blocks", c] = blocks

        return task

    split = factor.shape[1] // levels % 128 == 0
    table = arrivals(levels)

    def pick(values, dtype=jnp.int32):
        return lax.dynamic_index_in_dim(jnp.array(values, dtype), level, 0, keepdims=False)

    def place_of(part, window):
        if window is None:
            scalars = [level, core]
        elif window == 0:
            scalars = [level, jnp.zeros_like(level), core]
        else:
            came = [ways[window - 1] for ways in table]
            source = [i + (step if way == "down" else -step) for i, (way, step) in enumerate(came)]
            choice = [2 * (step - 1) + (way == "down") for way, step in came]
            scalars = [pick(source), pick(choice), core]
        return jnp.stack([(col + 1 + p) % col_size for p in range(*part)] + scalars).astype(jnp.int32)

    def multiply(c, part, window):
        def task():
            place = get(("place", c, part, window))
            if window is None:
                value = product(factor, get(("blocks", c)), levels, place, part[1] - part[0], rows)
            else:
                keys = [("own", c)] if window == 0 else []
                for step in range(1, window + 1):
                    keys += [("up", c, step), ("down", c, step)]
                blocks = []
                for key in keys:
                    blocks += [get(key), get(("swap",) + key)]
                total = line.values.get(("total", c))
                value = level_product(factor, blocks, total, place, part, rows)
            if window is None or window == levels - 1:
                line.values["product", c, part] = value
            else:
                put(("total", c), value, line.now + 1)

        return task

    def send_pieces(c, part, due):
        def task():
            value = get(("product", c, part))
            for p in range(*part):
                piece = value[p - part[0]]
                if p == col_size - 1:
                    line.values["kept", c] = piece
                else:
                    perm = [(i, (i + p + 1) % col_size) for i in range(col_size)]
                    coded = encode(piece)
                    put(("coded", c, p), coded, line.now + 1)
                    put(("got", c, p), lax.ppermute(coded, "col", perm), due)

        return task

    def add_pieces(c):
        def task():
            total = get(("kept", c))
            for p in range(col_size - 1):
                total = total + decode(get(("got", c, p)))
            line.values["image", c] = total
            images = [get(("image", i)) for i in range(c + 1)]
            line.values["so far", c] = jnp.concatenate(images, axis=1) if c else total

        return task

    stages = (
        ("row", CORES, core, lambda step: [(i, i // CORES * CORES + (i + step) % CORES) for i in range(row_size)]),
        ("col", col_size, col, lambda step: [(i, (i + step) % col_size) for i in range(col_size)]),
        ("row", levels, level, lambda step: [(i, (i + step * CORES) % row_size) for i in range(row_size)]),
    )

    def inner_products(c):
        def task():
            line.values["sum", c] = lax.dot_general(
                get(("so far", c)),
                get(("image", c)),
                (((0,), (0,)), ((), ())),
                precision=HIGHEST,
                preferred_element_type=jnp.float32,
            )

        return task

    def scatter_send(c, stage):
        def task():
            axis, size, index, perm = stages[stage]
            block = get(("sum", c))
            part = block.shape[0] // size
            for step in range(1, size):
                piece = lax.dynamic_slice_in_dim(block, (index + step) % size * part, part, 0)
                put(("add", c, step), lax.ppermute(piece, axis, perm(step)), line.now + 1)

        return task

    def scatter_add(c, stage):
        def task():
            _, size, index, _ = stages[stage]
            block = get(("sum", c))
            part = block.shape[0] // size
            total = lax.dynamic_slice_in_dim(block, index * part, part, 0)
            for step in range(1, size):
                total = total + get(("add", c, step))
            line.values["sum", c] = total

        return task

    def gather_send(c, stage):
        def task():
            axis, size, _, perm = stages[stage]
            for step in range(1, size):
                put(("add", c, step), lax.ppermute(get(("sum", c)), axis, perm(step)), line.now + 1)

        return task

    def gather_put(c, stage):
        def task():
            _, size, index, _ = stages[stage]
            block = get(("sum", c))
            part = block.shape[0]
            whole = jnp.zeros((size * part, block.shape[1]), block.dtype)
            whole = lax.dynamic_update_slice_in_dim(whole, block, index * part, 0)
            for step in range(1, size):
                whole = lax.dynamic_update_slice_in_dim(
                    whole, get(("add", c, step)), (index - step + size) % size * part, 0
                )
            line.values["sum", c] = whole

        return task


    def finish(c):
        def task():
            gram, inverse = get(("sum", c)), line.values.get("inverse")
            for low in range(0, WIDTHS[c], COLUMN):
                end = starts[c] + low + COLUMN
                column, last_rows = factor_column(gram[:end, low : low + COLUMN], inverse, 1.0 / total_rows)
                line.values["column", end] = jnp.pad(column, ((0, subspace.shape[1] - end), (0, 0)))
                if inverse is None:
                    inverse = last_rows
                else:
                    inverse = jnp.concatenate([jnp.pad(inverse, ((0, 0), (0, COLUMN))), last_rows], axis=0)
            line.values["inverse"] = inverse
            put(("last", c), inverse[starts[c] :], line.now + 1)

        return task

    def multiply_basis(c):
        def task():
            line.values["basis", c] = lax.dot_general(
                get(("so far", c)),
                get(("last", c)),
                (((1,), (1,)), ((), ())),
                precision=lax.Precision.HIGH,
                preferred_element_type=jnp.float32,
            )

        return task

    busy = 0
    for c in range(chunks):
        ready = max(arrival[c, levels - 1], busy)
        at(ready, assemble(c))
        everything = (0, col_size)
        for window in range(levels - 1 if split else 0):
            slot = sent[c, 1] if window == 0 else arrival[c, window]
            if c and window:
                slot = max(slot, arrival[c - 1, levels - 1] + 1)
            put(("place", c, everything, window), place_of(everything, window), slot)
            at(slot, multiply(c, everything, window))
        parts = parts_of(c)
        window = levels - 1 if split else None
        for i, part in enumerate(parts):
            put(("place", c, part, window), place_of(part, window), ready + i)
            at(ready + i, multiply(c, part, window))
        busy = ready + len(parts)
        slot = BASE[c] + busy
        for i, part in enumerate(parts):
            at(ready + i, send_pieces(c, part, slot))
        at(slot, add_pieces(c))
        at(slot, inner_products(c))
        for stage in range(len(stages)):
            at(slot, scatter_send(c, stage))
            at(slot + 1, scatter_add(c, stage))
            slot += 1
        for stage in reversed(range(len(stages))):
            at(slot, gather_send(c, stage))
            at(slot + 1, gather_put(c, stage))
            slot += 1
        at(slot, finish(c))
        at(slot + 1, multiply_basis(c))

    for slot in range(max(tasks) + 1):
        if slot:
            line.advance()
        for task in tasks.get(slot, []):
            task()
    basis = jnp.concatenate([get(("basis", c)) for c in range(chunks)], axis=1)
    upper = jnp.concatenate(
        [get(("column", end)) for end in range(COLUMN, subspace.shape[1] + 1, COLUMN)], axis=1
    )
    return basis, upper


def solution(mesh):
    row_size, col_size = mesh.shape["row"], mesh.shape["col"]
    return jax.shard_map(
        functools.partial(body, row_size, col_size),
        mesh=mesh,
        in_specs=(P("row", "col"), P(("col", "row"), None)),
        out_specs=(P(("row", "col"), None), P()),
        check_vma=False,
    )
```

```python
import functools

import jax
import jax.numpy as jnp
from jax import lax
from jax.experimental import pallas as pl
from jax.experimental.pallas import tpu as pltpu
from jax.sharding import PartitionSpec as P

WIDTHS = (512, 512)
COLUMN = 256
PIVOTS = 128
TILE = 8
BASE = (1, 1)
CORES = 2
ROW_TILE = 448
HIGHEST = lax.Precision.HIGHEST


class Timeline:
    def __init__(self):
        self.now = 0
        self.values = {}
        self.due = {}

    def put(self, key, value, at):
        self.values[key] = value
        self.due.setdefault(max(at, self.now + 1), []).append(key)

    def get(self, key):
        return self.values[key]

    def advance(self):
        self.now += 1
        keys = self.due.pop(self.now, [])
        passed = lax.optimization_barrier(tuple(self.values[k] for k in keys))
        self.values.update(zip(keys, passed))


def arrivals(levels):
    table = []
    for level in range(levels):
        came = []
        for step in range(1, levels):
            came += [("up", step)] if level >= step else []
            came += [("down", step)] if level + step < levels else []
        table.append(came)
    return table


def level_kernel(pieces, candidates, has_total, place_ref, factor_ref, *refs):
    blocks, (out_ref, panel_ref, sems) = refs[: 2 * candidates], refs[-3:]
    choice, core = place_ref[pieces + 1], place_ref[pieces + 2]
    rows = blocks[0].shape[0]

    @pl.when((pl.program_id(0) == 0) & (pl.program_id(1) == 0))
    def _():
        waits = []
        for swapped in range(2):
            start = pl.multiple_of(((1 - core) if swapped else core) * rows, 16)
            copies = [
                pltpu.make_async_copy(blocks[2 * k + swapped], panel_ref.at[pl.ds(start, rows)], sems.at[swapped])
                for k in range(candidates)
            ]
            for k, copy in enumerate(copies):

                @pl.when(choice == k)
                def _():
                    copy.start()

            waits.append(copies[0])
        for wait in waits:
            wait.wait()

    value = jnp.dot(factor_ref[...], panel_ref[...], preferred_element_type=jnp.float32)
    out_ref[0] = value + refs[2 * candidates][0] if has_total else value


def level_product(factor, blocks, total, place, part, rows):
    low, high = part
    pieces = high - low
    tile = rows
    while tile > ROW_TILE:
        tile //= 2
    per = rows // tile
    depth = CORES * rows
    width = blocks[0].shape[1]
    totals = [] if total is None else [total]
    whole = total is not None and total.shape[0] == pieces
    return pl.pallas_call(
        functools.partial(level_kernel, pieces, len(blocks) // 2, bool(totals)),
        out_shape=jax.ShapeDtypeStruct((pieces, rows, width), jnp.float32),
        grid_spec=pltpu.PrefetchScalarGridSpec(
            num_scalar_prefetch=1,
            grid=(pieces, per),
            in_specs=[pl.BlockSpec((tile, depth), lambda p, t, place: (place[p] * per + t, place[pieces]))]
            + [pl.BlockSpec(memory_space=pl.ANY)] * len(blocks)
            + [pl.BlockSpec((1, tile, width), lambda p, t, place: (p + low, t, 0))] * len(totals),
            out_specs=pl.BlockSpec((1, tile, width), lambda p, t, place: (p, t, 0)),
            scratch_shapes=[
                pltpu.VMEM((depth, width), factor.dtype),
                pltpu.SemaphoreType.DMA((2,)),
            ],
        ),
        input_output_aliases={2 + len(blocks): 0} if whole else {},
        compiler_params=pltpu.CompilerParams(vmem_limit_bytes=14 * 1024 * 1024),
        cost_estimate=pl.CostEstimate(
            flops=2 * pieces * rows * depth * width, bytes_accessed=2 * pieces * rows * depth, transcendentals=0
        ),
    )(place, factor, *blocks, *totals)


def product_kernel(levels, pieces, place_ref, factor_ref, *refs):
    blocks, (out_ref, panel_ref, sems) = refs[:-3], refs[-3:]
    level, core = place_ref[pieces], place_ref[pieces + 1]
    rows = blocks[0].shape[0]
    own, rising, falling = blocks[:2], blocks[2 : 2 * levels], blocks[2 * levels :]

    @pl.when((pl.program_id(0) == 0) & (pl.program_id(1) == 0))
    def _():
        def copy(block, slot, sem):
            start = pl.multiple_of(slot * rows, 16)
            return pltpu.make_async_copy(block, panel_ref.at[pl.ds(start, rows)], sems.at[sem])

        waits = []
        for swapped in range(2):
            at_core = (1 - core) if swapped else core
            first = copy(own[swapped], level * CORES + at_core, swapped)
            first.start()
            waits.append(first)
            for step in range(1, levels):
                slot = (level - step + levels) % levels * CORES + at_core
                sem = 2 * step + swapped
                below = copy(rising[2 * (step - 1) + swapped], slot, sem)
                above = copy(falling[2 * (levels - step - 1) + swapped], slot, sem)

                @pl.when(level >= step)
                def _():
                    below.start()

                @pl.when(level < step)
                def _():
                    above.start()

                waits.append(below)
        for wait in waits:
            wait.wait()

    out_ref[0] = jnp.dot(factor_ref[...], panel_ref[...], preferred_element_type=jnp.float32)


def product(factor, blocks, levels, place, pieces, rows):
    tile = rows
    while tile > ROW_TILE:
        tile //= 2
    per = rows // tile
    depth = factor.shape[1]
    width = blocks[0].shape[1]
    return pl.pallas_call(
        functools.partial(product_kernel, levels, pieces),
        out_shape=jax.ShapeDtypeStruct((pieces, rows, width), jnp.float32),
        grid_spec=pltpu.PrefetchScalarGridSpec(
            num_scalar_prefetch=1,
            grid=(pieces, per),
            in_specs=[pl.BlockSpec((tile, depth), lambda p, t, place: (place[p] * per + t, 0))]
            + [pl.BlockSpec(memory_space=pl.ANY)] * len(blocks),
            out_specs=pl.BlockSpec((1, tile, width), lambda p, t, place: (p, t, 0)),
            scratch_shapes=[
                pltpu.VMEM((depth, width), factor.dtype),
                pltpu.SemaphoreType.DMA((2 * levels,)),
            ],
        ),
        compiler_params=pltpu.CompilerParams(vmem_limit_bytes=30 * 1024 * 1024),
        cost_estimate=pl.CostEstimate(
            flops=2 * pieces * rows * depth * width, bytes_accessed=2 * pieces * rows * depth, transcendentals=0
        ),
    )(place, factor, *blocks)


def encode(piece):
    top = jnp.max(jnp.abs(piece), axis=0, keepdims=True)
    power = jnp.ceil(jnp.log2(jnp.maximum(top, 1e-30)))
    coded = (piece * jnp.exp2(14.0 - power)).astype(jnp.float16)
    tail = jnp.broadcast_to(power, (16, piece.shape[1])).astype(jnp.float16)
    return jnp.concatenate([coded, tail], axis=0)


def decode(sent):
    sent = sent.astype(jnp.float32)
    rows = sent.shape[0] - 16
    return sent[:rows] * jnp.exp2(sent[rows : rows + 1] - 14.0)


def inverse_of(x):
    guess = pl.reciprocal(x, approx=True)
    return guess * (2.0 - x * guess)


def eliminate(block):
    groups = PIVOTS // TILE
    shape = (TILE, PIVOTS)
    lane = lax.broadcasted_iota(jnp.int32, shape, 1)
    sub = lax.broadcasted_iota(jnp.int32, shape, 0)
    held = [block[g * TILE : (g + 1) * TILE] for g in range(groups)]
    factor, inverse = [], []
    for g in range(groups):
        base = g * TILE
        inside = (lane >= base) & (lane < base + TILE)
        rows = [jnp.broadcast_to(held[g][i : i + 1], shape) for i in range(TILE)]
        entry = [
            [jnp.broadcast_to(rows[i][:, base + j : base + j + 1], shape) if j >= i else None for j in range(TILE)]
            for i in range(TILE)
        ]
        upper = list(rows)
        unit = [jnp.where(inside, jnp.where(lane == base + i, 1.0, 0.0), rows[i]) for i in range(TILE)]
        pivot_inverse = []
        lower = [[None] * TILE for _ in range(TILE)]
        for k in range(TILE):
            pivot_inverse.append(inverse_of(entry[k][k]))
            for i in range(k + 1, TILE):
                weight = entry[k][i] * pivot_inverse[k]
                lower[i][k] = weight
                for j in range(i, TILE):
                    entry[i][j] = entry[i][j] - weight * entry[k][j]
                upper[i] = upper[i] - weight * upper[k]
                unit[i] = unit[i] - weight * unit[k]
        solved = [None] * TILE
        for k in reversed(range(TILE)):
            value = unit[k] * pivot_inverse[k]
            for i in range(k + 1, TILE):
                value = value - lower[i][k] * solved[i]
            solved[k] = value
        for h in range(g + 1, groups):
            old = held[h]
            new = jnp.where(inside, 0.0, old)
            for k in range(TILE):
                new = new - jnp.broadcast_to(old[:, base + k : base + k + 1], shape) * solved[k]
            held[h] = new
        diagonal, top, low = entry[0][0], upper[0], unit[0]
        for k in range(1, TILE):
            diagonal = jnp.where(sub == k, entry[k][k], diagonal)
            top = jnp.where(sub == k, upper[k], top)
            low = jnp.where(sub == k, unit[k], low)
        root = lax.rsqrt(diagonal)
        root = root * (1.5 - 0.5 * diagonal * root * root)
        own = sub + base
        factor.append(jnp.where(lane >= own, top * root, 0.0))
        inverse.append(jnp.where(lane <= own, low * root, 0.0))
    return jnp.concatenate(factor, 0), jnp.concatenate(inverse, 0)


def mul(a, b):
    return jnp.dot(a, b, precision=HIGHEST, preferred_element_type=jnp.float32)


def column_kernel(scale, before, width, gram_ref, *refs):
    factor_ref, inverse_ref = refs[-2:]
    block = gram_ref[before:, :] * scale
    if before:
        above = mul(refs[0][...], gram_ref[:before, :] * scale)
        factor_ref[:before, :] = above
        above_t = above.T
        block = block - mul(above_t, above)
    block = (block + block.T) * 0.5
    if width == PIVOTS:
        factor, inverse = eliminate(block)
    else:
        first, first_inverse = eliminate(block[:PIVOTS, :PIVOTS])
        corner = mul(first_inverse, block[:PIVOTS, PIVOTS:])
        corner_t = corner.T
        last, last_inverse = eliminate(block[PIVOTS:, PIVOTS:] - mul(corner_t, corner))
        low = -mul(last_inverse, mul(corner_t, first_inverse))
        none = jnp.zeros((PIVOTS, PIVOTS), jnp.float32)
        factor = jnp.concatenate(
            [jnp.concatenate([first, corner], 1), jnp.concatenate([none, last], 1)], 0
        )
        inverse = jnp.concatenate(
            [jnp.concatenate([first_inverse, none], 1), jnp.concatenate([low, last_inverse], 1)], 0
        )
    factor_ref[before:, :] = factor
    inverse_ref[:, before:] = inverse
    if before:
        inverse_ref[:, :before] = -mul(mul(inverse, above_t), refs[0][...])


def factor_column(gram, inverse_before, scale):
    width = gram.shape[1]
    before = gram.shape[0] - width
    operands = (gram,) if inverse_before is None else (gram, inverse_before)
    return pl.pallas_call(
        functools.partial(column_kernel, scale, before, width),
        out_shape=(
            jax.ShapeDtypeStruct((before + width, width), jnp.float32),
            jax.ShapeDtypeStruct((width, before + width), jnp.float32),
        ),
        in_specs=[pl.BlockSpec(memory_space=pltpu.VMEM)] * len(operands),
        out_specs=(pl.BlockSpec(memory_space=pltpu.VMEM),) * 2,
        compiler_params=pltpu.CompilerParams(vmem_limit_bytes=32 * 1024 * 1024),
        cost_estimate=pl.CostEstimate(flops=16_000_000_000, bytes_accessed=4_000_000, transcendentals=0),
    )(*operands)


def halves(x):
    high = x.astype(jnp.bfloat16)
    return high, (x - high.astype(jnp.float32)).astype(jnp.bfloat16)


def basis_kernel(x_ref, rows_ref, *refs):
    out_ref = refs[-1]
    x_high, x_low = halves(x_ref[...])
    w_high, w_low = halves(rows_ref[...])

    def nt(a, b):
        return lax.dot_general(a, b, (((1,), (1,)), ((), ())), preferred_element_type=jnp.float32)

    value = nt(x_high, w_high) + (nt(x_high, w_low) + nt(x_low, w_high))
    done = out_ref.shape[1] - value.shape[1]
    if done:
        out_ref[:, :done] = refs[0][...]
    out_ref[:, done:] = value


def basis_product(x, last_rows, before):
    rows, depth = x.shape
    tile = rows // 2 if rows % 32 == 0 else rows
    operands = (x, last_rows) if before is None else (x, last_rows, before)
    specs = [pl.BlockSpec((tile, depth), lambda i: (i, 0)), pl.BlockSpec(last_rows.shape, lambda i: (0, 0))]
    if before is not None:
        specs.append(pl.BlockSpec((tile, before.shape[1]), lambda i: (i, 0)))
    return pl.pallas_call(
        basis_kernel,
        out_shape=jax.ShapeDtypeStruct((rows, depth), jnp.float32),
        grid=(rows // tile,),
        in_specs=specs,
        out_specs=pl.BlockSpec((tile, depth), lambda i: (i, 0)),
        compiler_params=pltpu.CompilerParams(vmem_limit_bytes=32 * 1024 * 1024),
        cost_estimate=pl.CostEstimate(
            flops=6 * rows * depth * last_rows.shape[0], bytes_accessed=8 * rows * depth, transcendentals=0
        ),
    )(*operands)


def body(row_size, col_size, factor, subspace):
    rows = subspace.shape[0]
    total_rows = rows * row_size * col_size
    levels = row_size // CORES
    chunks = len(WIDTHS)
    starts = [sum(WIDTHS[:c]) for c in range(chunks)]
    row, col = lax.axis_index("row"), lax.axis_index("col")
    level, core = row // CORES, row % CORES
    up = [(i, i + CORES) for i in range(row_size - CORES)]
    down = [(i + CORES, i) for i in range(row_size - CORES)]
    swap = [(i, i // CORES * CORES + (i + 1) % CORES) for i in range(row_size)]

    line = Timeline()
    put, get = line.put, line.get
    tasks = {}

    def at(slot, task):
        tasks.setdefault(slot, []).append(task)

    sent = {(c, step): c * (levels - 2) + step - 1 for c in range(chunks) for step in range(1, levels)}
    arrival = {key: slot + 1 for key, slot in sent.items()}

    def send_line(c, step):
        def task():
            for way, perm in (("up", up), ("down", down)):
                source = get((way, c, step - 1)) if step > 1 else get(("own", c))
                put((way, c, step), lax.ppermute(source, "row", perm), arrival[c, step])

        return task

    def swap_cores(c, step):
        def task():
            for key in [("up", c, step), ("down", c, step)] if step else [("own", c)]:
                line.values[("swap",) + key] = lax.ppermute(get(key), "row", swap)

        return task

    for c, width in enumerate(WIDTHS):
        own = lax.slice_in_dim(subspace, starts[c], starts[c] + width, axis=1)
        put(("own", c), own, sent[c, 1])
        at(sent[c, 1], swap_cores(c, 0))
        for step in range(1, levels):
            at(sent[c, step], send_line(c, step))
            at(arrival[c, step], swap_cores(c, step))

    def parts_of(c):
        calls = min(1 if c < chunks - 1 else 2, col_size)
        return [(col_size * i // calls, col_size * (i + 1) // calls) for i in range(calls)]

    def assemble(c):
        def task():
            blocks = [get(("own", c)), get(("swap", "own", c))]
            for way in ("up", "down"):
                for step in range(1, levels):
                    blocks += [get((way, c, step)), get(("swap", way, c, step))]
            line.values["blocks", c] = blocks

        return task

    split = factor.shape[1] // levels % 128 == 0
    table = arrivals(levels)

    def pick(values, dtype=jnp.int32):
        return lax.dynamic_index_in_dim(jnp.array(values, dtype), level, 0, keepdims=False)

    def place_of(part, window):
        if window is None:
            scalars = [level, core]
        elif window == 0:
            scalars = [level, jnp.zeros_like(level), core]
        else:
            came = [ways[window - 1] for ways in table]
            source = [i + (step if way == "down" else -step) for i, (way, step) in enumerate(came)]
            choice = [2 * (step - 1) + (way == "down") for way, step in came]
            scalars = [pick(source), pick(choice), core]
        return jnp.stack([(col + 1 + p) % col_size for p in range(*part)] + scalars).astype(jnp.int32)

    def multiply(c, part, window):
        def task():
            place = get(("place", c, part, window))
            if window is None:
                value = product(factor, get(("blocks", c)), levels, place, part[1] - part[0], rows)
            else:
                keys = [("own", c)] if window == 0 else []
                for step in range(1, window + 1):
                    keys += [("up", c, step), ("down", c, step)]
                blocks = []
                for key in keys:
                    blocks += [get(key), get(("swap",) + key)]
                total = line.values.get(("total", c))
                value = level_product(factor, blocks, total, place, part, rows)
            if window is None or window == levels - 1:
                line.values["product", c, part] = value
            else:
                put(("total", c), value, line.now + 1)

        return task

    def send_pieces(c, part, due):
        def task():
            value = get(("product", c, part))
            for p in range(*part):
                piece = value[p - part[0]]
                if p == col_size - 1:
                    line.values["kept", c] = piece
                else:
                    perm = [(i, (i + p + 1) % col_size) for i in range(col_size)]
                    coded = encode(piece)
                    put(("coded", c, p), coded, line.now + 1)
                    put(("got", c, p), lax.ppermute(coded, "col", perm), due)

        return task

    def add_pieces(c):
        def task():
            total = get(("kept", c))
            for p in range(col_size - 1):
                total = total + decode(get(("got", c, p)))
            line.values["image", c] = total
            images = [get(("image", i)) for i in range(c + 1)]
            line.values["so far", c] = jnp.concatenate(images, axis=1) if c else total

        return task

    stages = (
        ("row", CORES, core, lambda step: [(i, i // CORES * CORES + (i + step) % CORES) for i in range(row_size)]),
        ("col", col_size, col, lambda step: [(i, (i + step) % col_size) for i in range(col_size)]),
        ("row", levels, level, lambda step: [(i, (i + step * CORES) % row_size) for i in range(row_size)]),
    )

    def inner_products(c):
        def task():
            line.values["sum", c] = lax.dot_general(
                get(("so far", c)),
                get(("image", c)),
                (((0,), (0,)), ((), ())),
                precision=lax.Precision.HIGH,
                preferred_element_type=jnp.float32,
            )

        return task

    def scatter_send(c, stage):
        def task():
            axis, size, index, perm = stages[stage]
            block = get(("sum", c))
            part = block.shape[0] // size
            for step in range(1, size):
                piece = lax.dynamic_slice_in_dim(block, (index + step) % size * part, part, 0)
                put(("add", c, step), lax.ppermute(piece, axis, perm(step)), line.now + 1)

        return task

    def scatter_add(c, stage):
        def task():
            _, size, index, _ = stages[stage]
            block = get(("sum", c))
            part = block.shape[0] // size
            total = lax.dynamic_slice_in_dim(block, index * part, part, 0)
            for step in range(1, size):
                total = total + get(("add", c, step))
            line.values["sum", c] = total

        return task

    def gather_send(c, stage):
        def task():
            axis, size, _, perm = stages[stage]
            for step in range(1, size):
                put(("add", c, step), lax.ppermute(get(("sum", c)), axis, perm(step)), line.now + 1)

        return task

    def gather_put(c, stage):
        def task():
            _, size, index, _ = stages[stage]
            block = get(("sum", c))
            part = block.shape[0]
            whole = jnp.zeros((size * part, block.shape[1]), block.dtype)
            whole = lax.dynamic_update_slice_in_dim(whole, block, index * part, 0)
            for step in range(1, size):
                whole = lax.dynamic_update_slice_in_dim(
                    whole, get(("add", c, step)), (index - step + size) % size * part, 0
                )
            line.values["sum", c] = whole

        return task


    def finish(c):
        def task():
            gram, inverse = get(("sum", c)), line.values.get("inverse")
            for low in range(0, WIDTHS[c], COLUMN):
                end = starts[c] + low + COLUMN
                column, last_rows = factor_column(gram[:end, low : low + COLUMN], inverse, 1.0 / total_rows)
                line.values["column", end] = jnp.pad(column, ((0, subspace.shape[1] - end), (0, 0)))
                if inverse is None:
                    inverse = last_rows
                else:
                    inverse = jnp.concatenate([jnp.pad(inverse, ((0, 0), (0, COLUMN))), last_rows], axis=0)
            line.values["inverse"] = inverse
            put(("last", c), inverse[starts[c] :], line.now + 1)

        return task

    def multiply_basis(c):
        def task():
            before = get(("basis", c - 1)) if c else None
            line.values["basis", c] = basis_product(get(("so far", c)), get(("last", c)), before)

        return task

    busy = 0
    for c in range(chunks):
        ready = max(arrival[c, levels - 1], busy)
        at(ready, assemble(c))
        everything = (0, col_size)
        for window in range(levels - 1 if split else 0):
            slot = sent[c, 1] if window == 0 else arrival[c, window]
            if c and window:
                slot = max(slot, arrival[c - 1, levels - 1] + 1)
            put(("place", c, everything, window), place_of(everything, window), slot)
            at(slot, multiply(c, everything, window))
        parts = parts_of(c)
        window = levels - 1 if split else None
        for i, part in enumerate(parts):
            put(("place", c, part, window), place_of(part, window), ready + i)
            at(ready + i, multiply(c, part, window))
        busy = ready + len(parts)
        slot = BASE[c] + busy
        for i, part in enumerate(parts):
            at(ready + i, send_pieces(c, part, slot))
        at(slot, add_pieces(c))
        at(slot, inner_products(c))
        for stage in range(len(stages)):
            at(slot, scatter_send(c, stage))
            at(slot + 1, scatter_add(c, stage))
            slot += 1
        for stage in reversed(range(len(stages))):
            at(slot, gather_send(c, stage))
            at(slot + 1, gather_put(c, stage))
            slot += 1
        at(slot, finish(c))
        at(slot + 1, multiply_basis(c))

    for slot in range(max(tasks) + 1):
        if slot:
            line.advance()
        for task in tasks.get(slot, []):
            task()
    basis = get(("basis", chunks - 1))
    upper = jnp.concatenate(
        [get(("column", end)) for end in range(COLUMN, subspace.shape[1] + 1, COLUMN)], axis=1
    )
    return basis, upper


def solution(mesh):
    row_size, col_size = mesh.shape["row"], mesh.shape["col"]
    return jax.shard_map(
        functools.partial(body, row_size, col_size),
        mesh=mesh,
        in_specs=(P("row", "col"), P(("col", "row"), None)),
        out_specs=(P(("row", "col"), None), P()),
        check_vma=False,
    )
```

```python
import functools

import jax
import jax.numpy as jnp
from jax import lax
from jax.experimental import pallas as pl
from jax.experimental.pallas import tpu as pltpu
from jax.sharding import PartitionSpec as P

WIDTHS = (512, 512)
COLUMN = 256
PIVOTS = 128
TILE = 8
BASE = (1, 1)
CORES = 2
ROW_TILE = 448
HIGHEST = lax.Precision.HIGHEST


class Timeline:
    def __init__(self):
        self.now = 0
        self.values = {}
        self.due = {}

    def put(self, key, value, at):
        self.values[key] = value
        self.due.setdefault(max(at, self.now + 1), []).append(key)

    def get(self, key):
        return self.values[key]

    def advance(self):
        self.now += 1
        keys = self.due.pop(self.now, [])
        passed = lax.optimization_barrier(tuple(self.values[k] for k in keys))
        self.values.update(zip(keys, passed))


def arrivals(levels):
    table = []
    for level in range(levels):
        came = []
        for step in range(1, levels):
            came += [("up", step)] if level >= step else []
            came += [("down", step)] if level + step < levels else []
        table.append(came)
    return table


def level_kernel(pieces, candidates, has_total, place_ref, factor_ref, *refs):
    blocks, (out_ref, panel_ref, sems) = refs[: 2 * candidates], refs[-3:]
    choice, core = place_ref[pieces + 1], place_ref[pieces + 2]
    rows = blocks[0].shape[0]

    @pl.when((pl.program_id(0) == 0) & (pl.program_id(1) == 0))
    def _():
        waits = []
        for swapped in range(2):
            start = pl.multiple_of(((1 - core) if swapped else core) * rows, 16)
            copies = [
                pltpu.make_async_copy(blocks[2 * k + swapped], panel_ref.at[pl.ds(start, rows)], sems.at[swapped])
                for k in range(candidates)
            ]
            for k, copy in enumerate(copies):

                @pl.when(choice == k)
                def _():
                    copy.start()

            waits.append(copies[0])
        for wait in waits:
            wait.wait()

    value = jnp.dot(factor_ref[...], panel_ref[...], preferred_element_type=jnp.float32)
    out_ref[0] = value + refs[2 * candidates][0] if has_total else value


def level_product(factor, blocks, total, place, part, rows):
    low, high = part
    pieces = high - low
    tile = rows
    while tile > ROW_TILE:
        tile //= 2
    per = rows // tile
    depth = CORES * rows
    width = blocks[0].shape[1]
    totals = [] if total is None else [total]
    whole = total is not None and total.shape[0] == pieces
    return pl.pallas_call(
        functools.partial(level_kernel, pieces, len(blocks) // 2, bool(totals)),
        out_shape=jax.ShapeDtypeStruct((pieces, rows, width), jnp.float32),
        grid_spec=pltpu.PrefetchScalarGridSpec(
            num_scalar_prefetch=1,
            grid=(pieces, per),
            in_specs=[pl.BlockSpec((tile, depth), lambda p, t, place: (place[p] * per + t, place[pieces]))]
            + [pl.BlockSpec(memory_space=pl.ANY)] * len(blocks)
            + [pl.BlockSpec((1, tile, width), lambda p, t, place: (p + low, t, 0))] * len(totals),
            out_specs=pl.BlockSpec((1, tile, width), lambda p, t, place: (p, t, 0)),
            scratch_shapes=[
                pltpu.VMEM((depth, width), factor.dtype),
                pltpu.SemaphoreType.DMA((2,)),
            ],
        ),
        input_output_aliases={2 + len(blocks): 0} if whole else {},
        compiler_params=pltpu.CompilerParams(vmem_limit_bytes=14 * 1024 * 1024),
        cost_estimate=pl.CostEstimate(
            flops=2 * pieces * rows * depth * width, bytes_accessed=2 * pieces * rows * depth, transcendentals=0
        ),
    )(place, factor, *blocks, *totals)


def product_kernel(levels, pieces, place_ref, factor_ref, *refs):
    blocks, (out_ref, panel_ref, sems) = refs[:-3], refs[-3:]
    level, core = place_ref[pieces], place_ref[pieces + 1]
    rows = blocks[0].shape[0]
    own, rising, falling = blocks[:2], blocks[2 : 2 * levels], blocks[2 * levels :]

    @pl.when((pl.program_id(0) == 0) & (pl.program_id(1) == 0))
    def _():
        def copy(block, slot, sem):
            start = pl.multiple_of(slot * rows, 16)
            return pltpu.make_async_copy(block, panel_ref.at[pl.ds(start, rows)], sems.at[sem])

        waits = []
        for swapped in range(2):
            at_core = (1 - core) if swapped else core
            first = copy(own[swapped], level * CORES + at_core, swapped)
            first.start()
            waits.append(first)
            for step in range(1, levels):
                slot = (level - step + levels) % levels * CORES + at_core
                sem = 2 * step + swapped
                below = copy(rising[2 * (step - 1) + swapped], slot, sem)
                above = copy(falling[2 * (levels - step - 1) + swapped], slot, sem)

                @pl.when(level >= step)
                def _():
                    below.start()

                @pl.when(level < step)
                def _():
                    above.start()

                waits.append(below)
        for wait in waits:
            wait.wait()

    out_ref[0] = jnp.dot(factor_ref[...], panel_ref[...], preferred_element_type=jnp.float32)


def product(factor, blocks, levels, place, pieces, rows):
    tile = rows
    while tile > ROW_TILE:
        tile //= 2
    per = rows // tile
    depth = factor.shape[1]
    width = blocks[0].shape[1]
    return pl.pallas_call(
        functools.partial(product_kernel, levels, pieces),
        out_shape=jax.ShapeDtypeStruct((pieces, rows, width), jnp.float32),
        grid_spec=pltpu.PrefetchScalarGridSpec(
            num_scalar_prefetch=1,
            grid=(pieces, per),
            in_specs=[pl.BlockSpec((tile, depth), lambda p, t, place: (place[p] * per + t, 0))]
            + [pl.BlockSpec(memory_space=pl.ANY)] * len(blocks),
            out_specs=pl.BlockSpec((1, tile, width), lambda p, t, place: (p, t, 0)),
            scratch_shapes=[
                pltpu.VMEM((depth, width), factor.dtype),
                pltpu.SemaphoreType.DMA((2 * levels,)),
            ],
        ),
        compiler_params=pltpu.CompilerParams(vmem_limit_bytes=30 * 1024 * 1024),
        cost_estimate=pl.CostEstimate(
            flops=2 * pieces * rows * depth * width, bytes_accessed=2 * pieces * rows * depth, transcendentals=0
        ),
    )(place, factor, *blocks)


def encode(piece):
    top = jnp.max(jnp.abs(piece), axis=0, keepdims=True)
    power = jnp.ceil(jnp.log2(jnp.maximum(top, 1e-30)))
    coded = (piece * jnp.exp2(14.0 - power)).astype(jnp.float16)
    tail = jnp.broadcast_to(power, (16, piece.shape[1])).astype(jnp.float16)
    return jnp.concatenate([coded, tail], axis=0)


def decode(sent):
    sent = sent.astype(jnp.float32)
    rows = sent.shape[0] - 16
    return sent[:rows] * jnp.exp2(sent[rows : rows + 1] - 14.0)


def inverse_of(x):
    guess = pl.reciprocal(x, approx=True)
    return guess * (2.0 - x * guess)


def eliminate(block):
    groups = PIVOTS // TILE
    shape = (TILE, PIVOTS)
    lane = lax.broadcasted_iota(jnp.int32, shape, 1)
    sub = lax.broadcasted_iota(jnp.int32, shape, 0)
    held = [block[g * TILE : (g + 1) * TILE] for g in range(groups)]
    factor, inverse = [], []
    for g in range(groups):
        base = g * TILE
        inside = (lane >= base) & (lane < base + TILE)
        rows = [jnp.broadcast_to(held[g][i : i + 1], shape) for i in range(TILE)]
        entry = [
            [jnp.broadcast_to(rows[i][:, base + j : base + j + 1], shape) if j >= i else None for j in range(TILE)]
            for i in range(TILE)
        ]
        upper = list(rows)
        unit = [jnp.where(inside, jnp.where(lane == base + i, 1.0, 0.0), rows[i]) for i in range(TILE)]
        pivot_inverse = []
        lower = [[None] * TILE for _ in range(TILE)]
        for k in range(TILE):
            pivot_inverse.append(inverse_of(entry[k][k]))
            for i in range(k + 1, TILE):
                weight = entry[k][i] * pivot_inverse[k]
                lower[i][k] = weight
                for j in range(i, TILE):
                    entry[i][j] = entry[i][j] - weight * entry[k][j]
                upper[i] = upper[i] - weight * upper[k]
                unit[i] = unit[i] - weight * unit[k]
        solved = [None] * TILE
        for k in reversed(range(TILE)):
            value = unit[k] * pivot_inverse[k]
            for i in range(k + 1, TILE):
                value = value - lower[i][k] * solved[i]
            solved[k] = value
        for h in range(g + 1, groups):
            old = held[h]
            new = jnp.where(inside, 0.0, old)
            for k in range(TILE):
                new = new - jnp.broadcast_to(old[:, base + k : base + k + 1], shape) * solved[k]
            held[h] = new
        diagonal, top, low = entry[0][0], upper[0], unit[0]
        for k in range(1, TILE):
            diagonal = jnp.where(sub == k, entry[k][k], diagonal)
            top = jnp.where(sub == k, upper[k], top)
            low = jnp.where(sub == k, unit[k], low)
        root = lax.rsqrt(diagonal)
        root = root * (1.5 - 0.5 * diagonal * root * root)
        own = sub + base
        factor.append(jnp.where(lane >= own, top * root, 0.0))
        inverse.append(jnp.where(lane <= own, low * root, 0.0))
    return jnp.concatenate(factor, 0), jnp.concatenate(inverse, 0)


def mul(a, b):
    return jnp.dot(a, b, precision=HIGHEST, preferred_element_type=jnp.float32)


def halves(x):
    high = x.astype(jnp.bfloat16)
    return high, (x - high.astype(jnp.float32)).astype(jnp.bfloat16)


def mul_halves(a, b):
    a_high, a_low = halves(a)
    b_high, b_low = halves(b)

    def nn(x, y):
        return jnp.dot(x, y, preferred_element_type=jnp.float32)

    return nn(a_high, b_high) + (nn(a_high, b_low) + nn(a_low, b_high))


def column_kernel(scale, before, width, gram_ref, *refs):
    factor_ref, inverse_ref = refs[-2:]
    block = gram_ref[before:, :] * scale
    if before:
        above = mul(refs[0][...], gram_ref[:before, :] * scale)
        factor_ref[:before, :] = above
        above_t = above.T
        block = block - mul(above_t, above)
    block = (block + block.T) * 0.5
    if width == PIVOTS:
        factor, inverse = eliminate(block)
    else:
        first, first_inverse = eliminate(block[:PIVOTS, :PIVOTS])
        corner = mul(first_inverse, block[:PIVOTS, PIVOTS:])
        corner_t = corner.T
        last, last_inverse = eliminate(block[PIVOTS:, PIVOTS:] - mul(corner_t, corner))
        low = -mul(last_inverse, mul(corner_t, first_inverse))
        none = jnp.zeros((PIVOTS, PIVOTS), jnp.float32)
        factor = jnp.concatenate(
            [jnp.concatenate([first, corner], 1), jnp.concatenate([none, last], 1)], 0
        )
        inverse = jnp.concatenate(
            [jnp.concatenate([first_inverse, none], 1), jnp.concatenate([low, last_inverse], 1)], 0
        )
    factor_ref[before:, :] = factor
    inverse_ref[:, before:] = inverse
    if before:
        inverse_ref[:, :before] = -mul_halves(mul(inverse, above_t), refs[0][...])


def factor_column(gram, inverse_before, scale):
    width = gram.shape[1]
    before = gram.shape[0] - width
    operands = (gram,) if inverse_before is None else (gram, inverse_before)
    return pl.pallas_call(
        functools.partial(column_kernel, scale, before, width),
        out_shape=(
            jax.ShapeDtypeStruct((before + width, width), jnp.float32),
            jax.ShapeDtypeStruct((width, before + width), jnp.float32),
        ),
        in_specs=[pl.BlockSpec(memory_space=pltpu.VMEM)] * len(operands),
        out_specs=(pl.BlockSpec(memory_space=pltpu.VMEM),) * 2,
        compiler_params=pltpu.CompilerParams(vmem_limit_bytes=32 * 1024 * 1024),
        cost_estimate=pl.CostEstimate(flops=16_000_000_000, bytes_accessed=4_000_000, transcendentals=0),
    )(*operands)


def basis_kernel(x_ref, rows_ref, *refs):
    out_ref = refs[-1]
    x_high, x_low = halves(x_ref[...])
    w_high, w_low = halves(rows_ref[...])

    def nt(a, b):
        return lax.dot_general(a, b, (((1,), (1,)), ((), ())), preferred_element_type=jnp.float32)

    value = nt(x_high, w_high) + (nt(x_high, w_low) + nt(x_low, w_high))
    done = out_ref.shape[1] - value.shape[1]
    if done:
        out_ref[:, :done] = refs[0][...]
    out_ref[:, done:] = value


def basis_product(x, last_rows, before):
    rows, depth = x.shape
    tile = rows // 2 if rows % 32 == 0 else rows
    operands = (x, last_rows) if before is None else (x, last_rows, before)
    specs = [pl.BlockSpec((tile, depth), lambda i: (i, 0)), pl.BlockSpec(last_rows.shape, lambda i: (0, 0))]
    if before is not None:
        specs.append(pl.BlockSpec((tile, before.shape[1]), lambda i: (i, 0)))
    return pl.pallas_call(
        basis_kernel,
        out_shape=jax.ShapeDtypeStruct((rows, depth), jnp.float32),
        grid=(rows // tile,),
        in_specs=specs,
        out_specs=pl.BlockSpec((tile, depth), lambda i: (i, 0)),
        compiler_params=pltpu.CompilerParams(vmem_limit_bytes=32 * 1024 * 1024),
        cost_estimate=pl.CostEstimate(
            flops=6 * rows * depth * last_rows.shape[0], bytes_accessed=8 * rows * depth, transcendentals=0
        ),
    )(*operands)


def body(row_size, col_size, factor, subspace):
    rows = subspace.shape[0]
    total_rows = rows * row_size * col_size
    levels = row_size // CORES
    chunks = len(WIDTHS)
    starts = [sum(WIDTHS[:c]) for c in range(chunks)]
    row, col = lax.axis_index("row"), lax.axis_index("col")
    level, core = row // CORES, row % CORES
    up = [(i, i + CORES) for i in range(row_size - CORES)]
    down = [(i + CORES, i) for i in range(row_size - CORES)]
    swap = [(i, i // CORES * CORES + (i + 1) % CORES) for i in range(row_size)]

    line = Timeline()
    put, get = line.put, line.get
    tasks = {}

    def at(slot, task):
        tasks.setdefault(slot, []).append(task)

    sent = {(c, step): c * (levels - 2) + step - 1 for c in range(chunks) for step in range(1, levels)}
    arrival = {key: slot + 1 for key, slot in sent.items()}

    def send_line(c, step):
        def task():
            for way, perm in (("up", up), ("down", down)):
                source = get((way, c, step - 1)) if step > 1 else get(("own", c))
                put((way, c, step), lax.ppermute(source, "row", perm), arrival[c, step])

        return task

    def swap_cores(c, step):
        def task():
            for key in [("up", c, step), ("down", c, step)] if step else [("own", c)]:
                line.values[("swap",) + key] = lax.ppermute(get(key), "row", swap)

        return task

    for c, width in enumerate(WIDTHS):
        own = lax.slice_in_dim(subspace, starts[c], starts[c] + width, axis=1)
        put(("own", c), own, sent[c, 1])
        at(sent[c, 1], swap_cores(c, 0))
        for step in range(1, levels):
            at(sent[c, step], send_line(c, step))
            at(arrival[c, step], swap_cores(c, step))

    def parts_of(c):
        calls = min(1 if c < chunks - 1 else 2, col_size)
        return [(col_size * i // calls, col_size * (i + 1) // calls) for i in range(calls)]

    def assemble(c):
        def task():
            blocks = [get(("own", c)), get(("swap", "own", c))]
            for way in ("up", "down"):
                for step in range(1, levels):
                    blocks += [get((way, c, step)), get(("swap", way, c, step))]
            line.values["blocks", c] = blocks

        return task

    split = factor.shape[1] // levels % 128 == 0
    table = arrivals(levels)

    def pick(values, dtype=jnp.int32):
        return lax.dynamic_index_in_dim(jnp.array(values, dtype), level, 0, keepdims=False)

    def place_of(part, window):
        if window is None:
            scalars = [level, core]
        elif window == 0:
            scalars = [level, jnp.zeros_like(level), core]
        else:
            came = [ways[window - 1] for ways in table]
            source = [i + (step if way == "down" else -step) for i, (way, step) in enumerate(came)]
            choice = [2 * (step - 1) + (way == "down") for way, step in came]
            scalars = [pick(source), pick(choice), core]
        return jnp.stack([(col + 1 + p) % col_size for p in range(*part)] + scalars).astype(jnp.int32)

    def multiply(c, part, window):
        def task():
            place = get(("place", c, part, window))
            if window is None:
                value = product(factor, get(("blocks", c)), levels, place, part[1] - part[0], rows)
            else:
                keys = [("own", c)] if window == 0 else []
                for step in range(1, window + 1):
                    keys += [("up", c, step), ("down", c, step)]
                blocks = []
                for key in keys:
                    blocks += [get(key), get(("swap",) + key)]
                total = line.values.get(("total", c))
                value = level_product(factor, blocks, total, place, part, rows)
            if window is None or window == levels - 1:
                line.values["product", c, part] = value
            else:
                put(("total", c), value, line.now + 1)

        return task

    def send_pieces(c, part, due):
        def task():
            value = get(("product", c, part))
            for p in range(*part):
                piece = value[p - part[0]]
                if p == col_size - 1:
                    line.values["kept", c] = piece
                else:
                    perm = [(i, (i + p + 1) % col_size) for i in range(col_size)]
                    coded = encode(piece)
                    put(("coded", c, p), coded, line.now + 1)
                    put(("got", c, p), lax.ppermute(coded, "col", perm), due)

        return task

    def add_pieces(c):
        def task():
            total = get(("kept", c))
            for p in range(col_size - 1):
                total = total + decode(get(("got", c, p)))
            line.values["image", c] = total
            images = [get(("image", i)) for i in range(c + 1)]
            line.values["so far", c] = jnp.concatenate(images, axis=1) if c else total

        return task

    stages = (
        ("row", CORES, core, lambda step: [(i, i // CORES * CORES + (i + step) % CORES) for i in range(row_size)]),
        ("col", col_size, col, lambda step: [(i, (i + step) % col_size) for i in range(col_size)]),
        ("row", levels, level, lambda step: [(i, (i + step * CORES) % row_size) for i in range(row_size)]),
    )

    def inner_products(c):
        def task():
            line.values["sum", c] = lax.dot_general(
                get(("so far", c)),
                get(("image", c)),
                (((0,), (0,)), ((), ())),
                precision=lax.Precision.HIGH,
                preferred_element_type=jnp.float32,
            )

        return task

    def scatter_send(c, stage):
        def task():
            axis, size, index, perm = stages[stage]
            block = get(("sum", c))
            part = block.shape[0] // size
            for step in range(1, size):
                piece = lax.dynamic_slice_in_dim(block, (index + step) % size * part, part, 0)
                put(("add", c, step), lax.ppermute(piece, axis, perm(step)), line.now + 1)

        return task

    def scatter_add(c, stage):
        def task():
            _, size, index, _ = stages[stage]
            block = get(("sum", c))
            part = block.shape[0] // size
            total = lax.dynamic_slice_in_dim(block, index * part, part, 0)
            for step in range(1, size):
                total = total + get(("add", c, step))
            line.values["sum", c] = total

        return task

    def gather_send(c, stage):
        def task():
            axis, size, _, perm = stages[stage]
            for step in range(1, size):
                put(("add", c, step), lax.ppermute(get(("sum", c)), axis, perm(step)), line.now + 1)

        return task

    def gather_put(c, stage):
        def task():
            _, size, index, _ = stages[stage]
            block = get(("sum", c))
            part = block.shape[0]
            whole = jnp.zeros((size * part, block.shape[1]), block.dtype)
            whole = lax.dynamic_update_slice_in_dim(whole, block, index * part, 0)
            for step in range(1, size):
                whole = lax.dynamic_update_slice_in_dim(
                    whole, get(("add", c, step)), (index - step + size) % size * part, 0
                )
            line.values["sum", c] = whole

        return task


    def finish(c):
        def task():
            gram, inverse = get(("sum", c)), line.values.get("inverse")
            for low in range(0, WIDTHS[c], COLUMN):
                end = starts[c] + low + COLUMN
                column, last_rows = factor_column(gram[:end, low : low + COLUMN], inverse, 1.0 / total_rows)
                line.values["column", end] = jnp.pad(column, ((0, subspace.shape[1] - end), (0, 0)))
                if inverse is None:
                    inverse = last_rows
                else:
                    inverse = jnp.concatenate([jnp.pad(inverse, ((0, 0), (0, COLUMN))), last_rows], axis=0)
            line.values["inverse"] = inverse
            put(("last", c), inverse[starts[c] :], line.now + 1)

        return task

    def multiply_basis(c):
        def task():
            before = get(("basis", c - 1)) if c else None
            line.values["basis", c] = basis_product(get(("so far", c)), get(("last", c)), before)

        return task

    busy = 0
    for c in range(chunks):
        ready = max(arrival[c, levels - 1], busy)
        at(ready, assemble(c))
        everything = (0, col_size)
        for window in range(levels - 1 if split else 0):
            slot = sent[c, 1] if window == 0 else arrival[c, window]
            if c and window:
                slot = max(slot, arrival[c - 1, levels - 1] + 1)
            put(("place", c, everything, window), place_of(everything, window), slot)
            at(slot, multiply(c, everything, window))
        parts = parts_of(c)
        window = levels - 1 if split else None
        for i, part in enumerate(parts):
            put(("place", c, part, window), place_of(part, window), ready + i)
            at(ready + i, multiply(c, part, window))
        busy = ready + len(parts)
        slot = BASE[c] + busy
        for i, part in enumerate(parts):
            at(ready + i, send_pieces(c, part, slot))
        at(slot, add_pieces(c))
        at(slot, inner_products(c))
        for stage in range(len(stages)):
            at(slot, scatter_send(c, stage))
            at(slot + 1, scatter_add(c, stage))
            slot += 1
        for stage in reversed(range(len(stages))):
            at(slot, gather_send(c, stage))
            at(slot + 1, gather_put(c, stage))
            slot += 1
        at(slot, finish(c))
        at(slot + 1, multiply_basis(c))

    for slot in range(max(tasks) + 1):
        if slot:
            line.advance()
        for task in tasks.get(slot, []):
            task()
    basis = get(("basis", chunks - 1))
    upper = jnp.concatenate(
        [get(("column", end)) for end in range(COLUMN, subspace.shape[1] + 1, COLUMN)], axis=1
    )
    return basis, upper


def solution(mesh):
    row_size, col_size = mesh.shape["row"], mesh.shape["col"]
    return jax.shard_map(
        functools.partial(body, row_size, col_size),
        mesh=mesh,
        in_specs=(P("row", "col"), P(("col", "row"), None)),
        out_specs=(P(("row", "col"), None), P()),
        check_vma=False,
    )
```
